32 devices in a mesh: space: 16 (over z, y, core), chan: 2 (over x).
Axes of the slice: x: 2, y: 2, z: 4, core: 2. Of those that a mesh axis runs over, the one named last changes fastest.
Arguments:
- field_in: bfloat16 [128, 512, 128], P('space', 'chan'), may hold values from -6 to 6
- kernel_first: bfloat16 [3, 3, 3, 512, 512], P(None, None, None, 'chan'), may hold values from -0.0546875 to 0.0546875
- bias_first: float32 [512], P('chan'), may hold values from -3 to 3
- kernel_second: bfloat16 [3, 3, 3, 512, 512], P(None, None, None, 'chan'), may hold values from -0.0546875 to 0.0546875
- bias_second: float32 [512], P('chan'), may hold values from -3 to 3
Outputs:
- field_out: bfloat16 [128, 512, 128], P('space', 'chan')
The draws below stay inside these ranges and needn't reach their ends.
All inputs are finite; a program needn't handle non-finite values.
Results may differ from the reference program's by a relative error of at most 0.0048.
Values may be sent and summed in bfloat16 or wider, within the bound.
A program may use at most 64 MiB of HBM per device.

```python
import jax
import jax.numpy as jnp
from jax import lax

C = 512
DILATION = 4
NY = 8
NX = 16
NZ = 128


def levels(key, shape, split, least, top_value):
    def one(dim, parts):
        draws = jax.random.uniform(jax.random.fold_in(jax.random.fold_in(key, 6), dim), (parts,), jnp.float32, least / len(split), top_value / len(split))
        return jnp.repeat(jnp.exp(draws), shape[dim] // parts).reshape((-1,) + (1,) * (len(shape) - dim - 1))

    factor_of = one(*split[0])
    for cut in split[1:]:
        factor_of = factor_of * one(*cut)
    return factor_of


def centred(rng, extent, spread, bound, shards=(), dtype=jnp.bfloat16):
    entries = jax.random.normal(rng, extent, jnp.float32) * spread
    if len(shards) > 0:
        entries = levels(rng, extent, shards, -0.22, 0.18) * entries
    return jnp.clip(entries, min=-bound, max=bound).astype(dtype)


def setup_inputs(seed: int = 0) -> dict:
    key_of = jax.random.split(jax.random.key(seed), 6)
    return {
        "field_in": centred(key_of[0], (NZ, C, NY * NX), 1.0, 6.0, ((0, 16), (1, 2))),
        "kernel_first": centred(key_of[1], (3, 3, 3, C, C), (27 * C) ** -0.5, 0.0546875, ((3, 2),)),
        "bias_first": centred(key_of[2], (C,), 0.5, 3.0, ((0, 2),), jnp.float32),
        "kernel_second": centred(key_of[3], (3, 3, 3, C, C), (27 * C) ** -0.5, 0.0546875, ((3, 2),)),
        "bias_second": centred(key_of[4], (C,), 0.5, 3.0, ((0, 2),), jnp.float32),
    }


def conv_block(field, kernel, bias):
    source = field.astype(jnp.float32)
    volume = jnp.transpose(source.reshape(source.shape[0], source.shape[1], NY, NX), (0, 2, 3, 1))
    taps = jnp.transpose(kernel.astype(jnp.float32), (0, 1, 2, 4, 3))
    pre = lax.conv_general_dilated(volume[None], taps, (1, 1, 1), [(DILATION, DILATION)] * 3, rhs_dilation=(DILATION, DILATION, DILATION), dimension_numbers=("NDHWC", "DHWIO", "NDHWC"), precision=lax.Precision.HIGHEST)[0]
    active = jax.nn.gelu(pre + bias, approximate=True)
    active = jnp.transpose(active, (0, 3, 1, 2)).reshape(source.shape)
    return (source + active).astype(jnp.bfloat16)


def reference(field_in, kernel_first, bias_first, kernel_second, bias_second):
    middle = conv_block(field_in, kernel_first, bias_first)
    return conv_block(middle, kernel_second, bias_second)
```

```python
import functools

import jax
import jax.numpy as jnp
from jax import lax
from jax.experimental import pallas as pl
from jax.experimental.pallas import tpu as pltpu
from jax.sharding import PartitionSpec as P

DILATION = 4
NX = 16
HALF = 64
LANES = 128
GROUPS = 2
MESH = pl.DeviceIdType.MESH


def kernel(
    ns, nc, field_ref, w1_hbm, b1_ref, w2_hbm, b2_ref, out_ref,
    planes, w1, w2, part, fin, w_sem, chan_send, chan_recv, halo_send, halo_recv,
):
    s = lax.axis_index("space")
    c = lax.axis_index("chan")
    local = field_ref.shape[1]
    full = local * nc
    has_prev = s > 0
    has_next = s < ns - 1
    prev = jnp.maximum(s - 1, 0)
    following = jnp.minimum(s + 1, ns - 1)

    def rows(owner):
        return pl.ds(pl.multiple_of(owner * local, local), local)

    weight_copies = [
        pltpu.make_async_copy(w1_hbm, w1, w_sem.at[0]),
        pltpu.make_async_copy(w2_hbm, w2, w_sem.at[1]),
    ]
    for copy in weight_copies:
        copy.start()

    barrier = pltpu.get_barrier_semaphore()
    for k in range(1, nc):
        pl.semaphore_signal(barrier, inc=1, device_id=(s, lax.rem(c + k, nc)), device_id_type=MESH)

    @pl.when(has_prev)
    def _():
        pl.semaphore_signal(barrier, inc=1, device_id=(prev, c), device_id_type=MESH)

    @pl.when(has_next)
    def _():
        pl.semaphore_signal(barrier, inc=1, device_id=(following, c), device_id_type=MESH)

    lane = lax.broadcasted_iota(jnp.int32, (local, LANES), 1)
    left = lane < HALF
    for g in range(GROUPS):
        for side in range(2):
            first = field_ref[4 * side + 2 * g].astype(jnp.float32)
            second = field_ref[4 * side + 2 * g + 1].astype(jnp.float32)
            low = jnp.where(left, first, pltpu.roll(second, HALF, 1))
            high = jnp.where(left, pltpu.roll(first, HALF, 1), second)
            planes[0, g, 1 + side, 0, rows(c), :] = low.astype(jnp.bfloat16)
            planes[0, g, 1 + side, 1, rows(c), :] = high.astype(jnp.bfloat16)

    @pl.when(jnp.logical_not(has_prev))
    def _():
        for conv in range(2):
            for g in range(GROUPS):
                planes[conv, g, 0] = jnp.zeros((2, full, LANES), jnp.bfloat16)

    @pl.when(jnp.logical_not(has_next))
    def _():
        for conv in range(2):
            for g in range(GROUPS):
                planes[conv, g, 3] = jnp.zeros((2, full, LANES), jnp.bfloat16)

    pl.semaphore_wait(barrier, nc - 1 + has_prev.astype(jnp.int32) + has_next.astype(jnp.int32))

    def chan_copy(conv, g, side, k):
        where = planes.at[conv, g, 1 + side, :, rows(c), :]
        return pltpu.make_async_remote_copy(
            src_ref=where, dst_ref=where,
            send_sem=chan_send.at[conv, g, side, k], recv_sem=chan_recv.at[conv, g, side, k],
            device_id=(s, lax.rem(c + k, nc)), device_id_type=MESH,
        )

    def chan_arrival(conv, g, side, k):
        owner = lax.rem(c - k + nc, nc)
        where = planes.at[conv, g, 1 + side, :, rows(owner), :]
        return pltpu.make_async_remote_copy(
            src_ref=where, dst_ref=where,
            send_sem=chan_send.at[conv, g, side, k], recv_sem=chan_recv.at[conv, g, side, k],
            device_id=(s, lax.rem(c + k, nc)), device_id_type=MESH,
        )

    def halo_copy(conv, g, side, k):
        owner = lax.rem(c - k + nc, nc)
        return pltpu.make_async_remote_copy(
            src_ref=planes.at[conv, g, 1 + side, :, rows(owner), :],
            dst_ref=planes.at[conv, g, 0 if side == 1 else 3, :, rows(owner), :],
            send_sem=halo_send.at[conv, g, side, k], recv_sem=halo_recv.at[conv, g, side, k],
            device_id=(following if side == 1 else prev, c), device_id_type=MESH,
        )

    def send_halo(conv, g, side, k):
        @pl.when(has_next if side == 1 else has_prev)
        def _():
            halo_copy(conv, g, side, k).start()

    def send_own(conv, g):
        for side in range(2):
            for k in range(1, nc):
                chan_copy(conv, g, side, k).start()
        for side in range(2):
            send_halo(conv, g, side, 0)

    def pass_on(conv, g):
        for side in range(2):
            for k in range(1, nc):
                chan_arrival(conv, g, side, k).wait_recv()
                send_halo(conv, g, side, k)

    def wait_halos(conv, g):
        for side in range(2):
            @pl.when(has_prev if side == 1 else has_next)
            def _():
                for k in range(nc):
                    halo_copy(conv, g, side, k).wait_recv()

    def wait_sends(conv, g):
        for side in range(2):
            for k in range(1, nc):
                chan_copy(conv, g, side, k).wait_send()

            @pl.when(has_next if side == 1 else has_prev)
            def _():
                for k in range(nc):
                    halo_copy(conv, g, side, k).wait_send()

    lane_x = lax.rem(lane, NX)
    from_left = lane_x >= DILATION
    from_right = lane_x < NX - DILATION

    def convolve(conv, g, taps, bias, store):
        for half in range(2):
            for dx in range(3):
                total = None
                for dz in range(3):
                    for other in range(2):
                        window = jnp.concatenate(
                            [planes[conv, g, dz, other], planes[conv, g, dz + 1, other]], axis=1
                        )
                        term = jnp.dot(
                            taps[dz, other - half + 1, dx], window, preferred_element_type=jnp.float32
                        )
                        total = term if total is None else total + term
                part[dx] = total
            for side in range(2):
                cols = pl.ds(side * LANES, LANES)
                pre = part[1, :, cols] + bias
                pre += jnp.where(from_left, pltpu.roll(part[0, :, cols], DILATION, 1), 0.0)
                pre += jnp.where(from_right, pltpu.roll(part[2, :, cols], LANES - DILATION, 1), 0.0)
                value = planes[conv, g, 1 + side, half, rows(c), :].astype(jnp.float32)
                value += jax.nn.gelu(pre, approximate=True)
                store(g, side, half, value)

    def keep(g, side, half, value):
        planes[1, g, 1 + side, half, rows(c), :] = value.astype(jnp.bfloat16)

    def finish(g, side, half, value):
        if half == 0:
            fin[side] = value
        else:
            low = fin[side]
            first = jnp.where(left, low, pltpu.roll(value, HALF, 1))
            second = jnp.where(left, pltpu.roll(low, HALF, 1), value)
            out_ref[4 * side + 2 * g] = first.astype(jnp.bfloat16)
            out_ref[4 * side + 2 * g + 1] = second.astype(jnp.bfloat16)

    for g in range(GROUPS):
        send_own(0, g)
    for conv, (taps, b_ref) in enumerate(((w1, b1_ref), (w2, b2_ref))):
        bias = jnp.transpose(jnp.broadcast_to(b_ref[...], (LANES, local)))
        weight_copies[conv].wait()
        for g in range(GROUPS):
            pass_on(conv, g)
            wait_halos(conv, g)
            convolve(conv, g, taps, bias, keep if conv == 0 else finish)
            if conv == 0:
                send_own(1, g)
    for conv in range(2):
        for g in range(GROUPS):
            wait_sends(conv, g)


def per_device(ns, nc, field_in, kernel_first, bias_first, kernel_second, bias_second):
    layers, local, voxels = field_in.shape
    full = local * nc
    vmem = pl.BlockSpec(memory_space=pltpu.VMEM)
    hbm = pl.BlockSpec(memory_space=pl.ANY)
    dma = pltpu.SemaphoreType.DMA
    return pl.pallas_call(
        functools.partial(kernel, ns, nc),
        out_shape=jax.ShapeDtypeStruct(field_in.shape, jnp.bfloat16),
        in_specs=[vmem, hbm, vmem, hbm, vmem],
        out_specs=vmem,
        scratch_shapes=[
            pltpu.VMEM((2, GROUPS, 4, 2, full, LANES), jnp.bfloat16),
            pltpu.VMEM(kernel_first.shape, jnp.bfloat16),
            pltpu.VMEM(kernel_second.shape, jnp.bfloat16),
            pltpu.VMEM((3, local, 2 * LANES), jnp.float32),
            pltpu.VMEM((2, local, LANES), jnp.float32),
            dma((2,)),
            dma((2, GROUPS, 2, nc)),
            dma((2, GROUPS, 2, nc)),
            dma((2, GROUPS, 2, nc)),
            dma((2, GROUPS, 2, nc)),
        ],
        cost_estimate=pl.CostEstimate(
            flops=2 * 2 * 27 * local * full * layers * voxels,
            bytes_accessed=2 * 27 * local * full * 2,
            transcendentals=2 * layers * local * voxels,
        ),
        compiler_params=pltpu.CompilerParams(
            collective_id=0, has_side_effects=True, vmem_limit_bytes=48 * 1024 * 1024
        ),
    )(field_in, kernel_first, bias_first.reshape(1, local), kernel_second, bias_second.reshape(1, local))


def solution(mesh):
    placed = (
        P("space", "chan", None),
        P(None, None, None, "chan", None),
        P("chan"),
        P(None, None, None, "chan", None),
        P("chan"),
    )
    body = functools.partial(per_device, mesh.shape["space"], mesh.shape["chan"])
    return jax.shard_map(
        body, mesh=mesh, in_specs=placed, out_specs=P("space", "chan", None), check_vma=False
    )
```

```python
import functools

import jax
import jax.numpy as jnp
from jax import lax
from jax.experimental import pallas as pl
from jax.experimental.pallas import tpu as pltpu
from jax.sharding import PartitionSpec as P

DILATION = 4
NX = 16
HALF = 64
LANES = 128
GROUPS = 2
MESH = pl.DeviceIdType.MESH


def kernel(
    ns, nc, field_hbm, w1_hbm, b1_hbm, w2_hbm, b2_hbm, out_ref,
    planes, w1, w2, part, field, b1, b2, border_out, border_in, fin,
    load_sem, chan_send, chan_recv, halo_send, halo_recv,
):
    s = lax.axis_index("space")
    c = lax.axis_index("chan")
    local = field.shape[1]
    has_prev = s > 0
    has_next = s < ns - 1
    prev = jnp.maximum(s - 1, 0)
    following = jnp.minimum(s + 1, ns - 1)
    split = local % LANES == 0

    def rows(owner):
        return pl.ds(pl.multiple_of(owner * local, local), local)

    barrier = pltpu.get_barrier_semaphore()
    for k in range(1, nc):
        pl.semaphore_signal(barrier, inc=1, device_id=(s, lax.rem(c + k, nc)), device_id_type=MESH)

    @pl.when(has_prev)
    def _():
        pl.semaphore_signal(barrier, inc=1, device_id=(prev, c), device_id_type=MESH)

    @pl.when(has_next)
    def _():
        pl.semaphore_signal(barrier, inc=1, device_id=(following, c), device_id_type=MESH)

    loads = [
        pltpu.make_async_copy(source, target, load_sem.at[n])
        for n, (source, target) in enumerate(
            ((field_hbm, field), (b1_hbm, b1), (b2_hbm, b2), (w1_hbm, w1), (w2_hbm, w2))
        )
    ]
    for load in loads:
        load.start()

    lane = lax.broadcasted_iota(jnp.int32, (local, LANES), 1)
    left = lane < HALF
    lane_x = lax.rem(lane, NX)
    from_left = lane_x >= DILATION
    from_right = lane_x < NX - DILATION

    def chan_copy(conv, g, k, owner):
        where = planes.at[conv, g, :, :, rows(owner), :]
        return pltpu.make_async_remote_copy(
            src_ref=where, dst_ref=where,
            send_sem=chan_send.at[conv, g, k], recv_sem=chan_recv.at[conv, g, k],
            device_id=(s, lax.rem(c + k, nc)), device_id_type=MESH,
        )

    def halo_copy(conv, g, up):
        return pltpu.make_async_remote_copy(
            src_ref=border_out.at[conv, g, up], dst_ref=border_in.at[conv, g, 1 - up],
            send_sem=halo_send.at[conv, g, up], recv_sem=halo_recv.at[conv, g, up],
            device_id=(following if up == 1 else prev, c), device_id_type=MESH,
        )

    def send_own(conv, g):
        for k in range(1, nc):
            chan_copy(conv, g, k, c).start()

    def wait_chan(conv, g):
        for k in range(1, nc):
            chan_copy(conv, g, k, lax.rem(c - k + nc, nc)).wait_recv()

    def send_halo(conv, g):
        for up in range(2):
            @pl.when(has_next if up == 1 else has_prev)
            def _():
                halo_copy(conv, g, up).start()

    def wait_halo(conv, g):
        for up in range(2):
            @pl.when(has_prev if up == 1 else has_next)
            def _():
                halo_copy(conv, g, up).wait_recv()

    def wait_sends(conv, g):
        for k in range(1, nc):
            chan_copy(conv, g, k, c).wait_send()
        for up in range(2):
            @pl.when(has_next if up == 1 else has_prev)
            def _():
                halo_copy(conv, g, up).wait_send()

    def multiply(conv, g, dz, taps, block, first):
        for half in range(2):
            total = None
            for other in range(2):
                window = jnp.concatenate(
                    [planes[conv, g, 0, other, block, :], planes[conv, g, 1, other, block, :]], axis=1
                )
                stack = taps[dz, other - half + 1, :, :, block]
                term = jnp.dot(
                    stack.reshape(3 * local, window.shape[0]), window, preferred_element_type=jnp.float32
                )
                total = term if total is None else total + term
            total = total.reshape(3, local, 2 * LANES)
            if first:
                part[g, dz, half] = total
            else:
                part[g, dz, half] += total

    def shifted(pick):
        value = pick(1)
        value += jnp.where(from_left, pltpu.roll(pick(0), DILATION, 1), 0.0)
        return value + jnp.where(from_right, pltpu.roll(pick(2), LANES - DILATION, 1), 0.0)

    lo, hi = pl.ds(0, LANES), pl.ds(LANES, LANES)

    def multiply_own(conv, g, taps):
        if split:
            for dz in (0, 2, 1):
                multiply(conv, g, dz, taps, rows(c), True)

    def multiply_rest(conv, g, taps):
        if split:
            blocks = [rows(lax.rem(c - k + nc, nc)) for k in range(1, nc)]
        else:
            blocks = [pl.ds(0, local * nc)]
        for dz in (0, 2, 1):
            for n, block in enumerate(blocks):
                multiply(conv, g, dz, taps, block, n == 0 and not split)
            if dz == 1:
                continue
            up, cols = (1, hi) if dz == 0 else (0, lo)
            for half in range(2):
                value = shifted(lambda dx: part[g, dz, half, dx, :, cols])
                border_out[conv, g, up, half] = value.astype(jnp.bfloat16)

            @pl.when(has_next if up == 1 else has_prev)
            def _():
                halo_copy(conv, g, up).start()

    def conclude(conv, g, bias, store):
        for side in range(2):
            dz, mine, cross = (2, lo, hi) if side == 0 else (0, hi, lo)
            for half in range(2):
                pre = shifted(lambda dx: part[g, 1, half, dx, :, mine] + part[g, dz, half, dx, :, cross])
                pre += border_in[conv, g, side, half].astype(jnp.float32) + bias
                value = planes[conv, g, side, half, rows(c), :].astype(jnp.float32)
                value += jax.nn.gelu(pre, approximate=True)
                store(g, side, half, value)

    def keep(g, side, half, value):
        planes[1, g, side, half, rows(c), :] = value.astype(jnp.bfloat16)

    def finish(g, side, half, value):
        if half == 0:
            fin[...] = value
        else:
            low = fin[...]
            first = jnp.where(left, low, pltpu.roll(value, HALF, 1))
            second = jnp.where(left, pltpu.roll(low, HALF, 1), value)
            out_ref[4 * side + 2 * g] = first.astype(jnp.bfloat16)
            out_ref[4 * side + 2 * g + 1] = second.astype(jnp.bfloat16)

    def pack(g):
        for side in range(2):
            first = field[4 * side + 2 * g].astype(jnp.float32)
            second = field[4 * side + 2 * g + 1].astype(jnp.float32)
            low = jnp.where(left, first, pltpu.roll(second, HALF, 1))
            high = jnp.where(left, pltpu.roll(first, HALF, 1), second)
            planes[0, g, side, 0, rows(c), :] = low.astype(jnp.bfloat16)
            planes[0, g, side, 1, rows(c), :] = high.astype(jnp.bfloat16)

    loads[0].wait()
    pack(0)
    pl.semaphore_wait(barrier, nc - 1 + has_prev.astype(jnp.int32) + has_next.astype(jnp.int32))
    send_own(0, 0)
    pack(1)
    send_own(0, 1)

    @pl.when(jnp.logical_not(has_prev))
    def _():
        for conv in range(2):
            for g in range(GROUPS):
                border_in[conv, g, 0] = jnp.zeros((2, local, LANES), jnp.bfloat16)

    @pl.when(jnp.logical_not(has_next))
    def _():
        for conv in range(2):
            for g in range(GROUPS):
                border_in[conv, g, 1] = jnp.zeros((2, local, LANES), jnp.bfloat16)

    loads[1].wait()
    loads[2].wait()
    bias1 = jnp.transpose(jnp.broadcast_to(b1[...], (LANES, local)))
    bias2 = jnp.transpose(jnp.broadcast_to(b2[...], (LANES, local)))
    loads[3].wait()
    multiply_own(0, 0, w1)
    multiply_own(0, 1, w1)
    wait_chan(0, 0)
    multiply_rest(0, 0, w1)
    loads[4].wait()
    wait_halo(0, 0)
    conclude(0, 0, bias1, keep)
    send_own(1, 0)
    wait_chan(0, 1)
    multiply_rest(0, 1, w1)
    multiply_own(1, 0, w2)
    wait_halo(0, 1)
    conclude(0, 1, bias1, keep)
    send_own(1, 1)
    multiply_own(1, 1, w2)
    for g in range(GROUPS):
        wait_chan(1, g)
        multiply_rest(1, g, w2)
        wait_halo(1, g)
        conclude(1, g, bias2, finish)
    for conv in range(2):
        for g in range(GROUPS):
            wait_sends(conv, g)


def per_device(ns, nc, field_in, kernel_first, bias_first, kernel_second, bias_second):
    layers, local, voxels = field_in.shape
    full = local * nc
    hbm = pl.BlockSpec(memory_space=pltpu.HBM)
    dma = pltpu.SemaphoreType.DMA
    border = pltpu.VMEM((2, GROUPS, 2, 2, local, LANES), jnp.bfloat16)
    return pl.pallas_call(
        functools.partial(kernel, ns, nc),
        out_shape=jax.ShapeDtypeStruct(field_in.shape, jnp.bfloat16),
        in_specs=[hbm] * 5,
        out_specs=pl.BlockSpec(memory_space=pltpu.VMEM),
        scratch_shapes=[
            pltpu.VMEM((2, GROUPS, 2, 2, full, LANES), jnp.bfloat16),
            pltpu.VMEM(kernel_first.shape, jnp.bfloat16),
            pltpu.VMEM(kernel_second.shape, jnp.bfloat16),
            pltpu.VMEM((GROUPS, 3, 2, 3, local, 2 * LANES), jnp.float32),
            pltpu.VMEM(field_in.shape, jnp.bfloat16),
            pltpu.VMEM((1, local), jnp.float32),
            pltpu.VMEM((1, local), jnp.float32),
            border,
            border,
            pltpu.VMEM((local, LANES), jnp.float32),
            dma((5,)),
            dma((2, GROUPS, nc)),
            dma((2, GROUPS, nc)),
            dma((2, GROUPS, 2)),
            dma((2, GROUPS, 2)),
        ],
        cost_estimate=pl.CostEstimate(
            flops=2 * 2 * 27 * local * full * layers * voxels,
            bytes_accessed=2 * 27 * local * full * 2,
            transcendentals=2 * layers * local * voxels,
        ),
        compiler_params=pltpu.CompilerParams(
            collective_id=0, has_side_effects=True, vmem_limit_bytes=50 * 1024 * 1024
        ),
    )(field_in, kernel_first, bias_first.reshape(1, local), kernel_second, bias_second.reshape(1, local))


def solution(mesh):
    placed = (
        P("space", "chan", None),
        P(None, None, None, "chan", None),
        P("chan"),
        P(None, None, None, "chan", None),
        P("chan"),
    )
    body = functools.partial(per_device, mesh.shape["space"], mesh.shape["chan"])
    return jax.shard_map(
        body, mesh=mesh, in_specs=placed, out_specs=P("space", "chan", None), check_vma=False
    )
```

```python
import functools

import jax
import jax.numpy as jnp
from jax import lax
from jax.experimental import pallas as pl
from jax.experimental.pallas import tpu as pltpu
from jax.sharding import PartitionSpec as P

DILATION = 4
NX = 16
HALF = 64
LANES = 128
GROUPS = 4
MESH = pl.DeviceIdType.MESH


def kernel(
    ns, nc, field_hbm, w1_hbm, b1_hbm, w2_hbm, b2_hbm, out_ref,
    planes, w1, w2, part, field, b1, b2, border_out, border_in,
    load_sem, chan_send, chan_recv, halo_send, halo_recv,
):
    s = lax.axis_index("space")
    c = lax.axis_index("chan")
    local = field.shape[1]
    has_prev = s > 0
    has_next = s < ns - 1
    prev = jnp.maximum(s - 1, 0)
    following = jnp.minimum(s + 1, ns - 1)
    split = local % LANES == 0

    def rows(owner):
        return pl.ds(pl.multiple_of(owner * local, local), local)

    barrier = pltpu.get_barrier_semaphore()
    for k in range(1, nc):
        pl.semaphore_signal(barrier, inc=1, device_id=(s, lax.rem(c + k, nc)), device_id_type=MESH)

    @pl.when(has_prev)
    def _():
        pl.semaphore_signal(barrier, inc=1, device_id=(prev, c), device_id_type=MESH)

    @pl.when(has_next)
    def _():
        pl.semaphore_signal(barrier, inc=1, device_id=(following, c), device_id_type=MESH)

    loads = [
        pltpu.make_async_copy(source, target, load_sem.at[n])
        for n, (source, target) in enumerate(
            ((field_hbm, field), (b1_hbm, b1), (b2_hbm, b2), (w1_hbm, w1), (w2_hbm, w2))
        )
    ]
    for load in loads:
        load.start()

    lane = lax.broadcasted_iota(jnp.int32, (local, LANES), 1)
    left = lane < HALF
    lane_x = lax.rem(lane, NX)
    from_left = lane_x >= DILATION
    from_right = lane_x < NX - DILATION

    def chan_copy(conv, g, k, owner):
        where = planes.at[conv, g, :, rows(owner), :]
        return pltpu.make_async_remote_copy(
            src_ref=where, dst_ref=where,
            send_sem=chan_send.at[conv, g, k], recv_sem=chan_recv.at[conv, g, k],
            device_id=(s, lax.rem(c + k, nc)), device_id_type=MESH,
        )

    def halo_copy(conv, g, up):
        return pltpu.make_async_remote_copy(
            src_ref=border_out.at[conv, g, up], dst_ref=border_in.at[conv, g, 1 - up],
            send_sem=halo_send.at[conv, g, up], recv_sem=halo_recv.at[conv, g, up],
            device_id=(following if up == 1 else prev, c), device_id_type=MESH,
        )

    def send_own(conv, g):
        for k in range(1, nc):
            chan_copy(conv, g, k, c).start()

    def wait_chan(conv, g):
        for k in range(1, nc):
            chan_copy(conv, g, k, lax.rem(c - k + nc, nc)).wait_recv()

    def wait_halo(conv, g):
        for up in range(2):
            @pl.when(has_prev if up == 1 else has_next)
            def _():
                halo_copy(conv, g, up).wait_recv()

    def wait_sends(conv, g):
        for k in range(1, nc):
            chan_copy(conv, g, k, c).wait_send()
        for up in range(2):
            @pl.when(has_next if up == 1 else has_prev)
            def _():
                halo_copy(conv, g, up).wait_send()

    def multiply(conv, g, dz, taps, block, first):
        low, high = planes[conv, g, 0, block, :], planes[conv, g, 1, block, :]

        def product(dy, window):
            stack = taps[dz, dy, :, :, block].reshape(3 * local, window.shape[0])
            return jnp.dot(stack, window, preferred_element_type=jnp.float32)

        both = product(1, jnp.concatenate([low, high], axis=1))
        for half, term in ((0, product(2, high)), (1, product(0, low))):
            total = both[:, half * LANES : (half + 1) * LANES] + term
            total = total.reshape(3, local, LANES)
            if first:
                part[g, dz, half] = total
            else:
                part[g, dz, half] += total

    def swapped(value):
        return pltpu.roll(value, HALF, 1)

    def exchanged(first, second):
        return jnp.where(left, first, swapped(second)), jnp.where(left, swapped(first), second)

    def shifted(pick):
        value = pick(1)
        value += jnp.where(from_left, pltpu.roll(pick(0), DILATION, 1), 0.0)
        return value + jnp.where(from_right, pltpu.roll(pick(2), LANES - DILATION, 1), 0.0)

    def multiply_own(conv, g, taps):
        if split:
            for dz in (0, 2, 1):
                multiply(conv, g, dz, taps, rows(c), True)

    def multiply_rest(conv, g, taps):
        if split:
            blocks = [rows(lax.rem(c - k + nc, nc)) for k in range(1, nc)]
        else:
            blocks = [pl.ds(0, local * nc)]
        for dz in (0, 2, 1):
            for n, block in enumerate(blocks):
                multiply(conv, g, dz, taps, block, n == 0 and not split)
            if dz != 2:
                continue
            outer = [
                shifted(lambda dx: jnp.where(left, part[g, 2, half, dx], part[g, 0, half, dx]))
                for half in range(2)
            ]
            for up, value in enumerate(exchanged(*outer)):
                border_out[conv, g, up] = value.astype(jnp.bfloat16)
            for up in range(2):
                @pl.when(has_next if up == 1 else has_prev)
                def _():
                    halo_copy(conv, g, up).start()

    def conclude(conv, g, bias, store):
        wait_halo(conv, g)
        arrived = exchanged(
            border_in[conv, g, 0].astype(jnp.float32), border_in[conv, g, 1].astype(jnp.float32)
        )
        values = []
        for half in range(2):
            pre = shifted(
                lambda dx: part[g, 1, half, dx]
                + swapped(jnp.where(left, part[g, 0, half, dx], part[g, 2, half, dx]))
            )
            pre += arrived[half] + bias
            value = planes[conv, g, half, rows(c), :].astype(jnp.float32)
            values.append(value + jax.nn.gelu(pre, approximate=True))
        store(g, values)

    def keep(g, values):
        for half in range(2):
            planes[1, g, half, rows(c), :] = values[half].astype(jnp.bfloat16)

    def finish(g, values):
        for side, value in enumerate(exchanged(*values)):
            out_ref[4 * side + g] = value.astype(jnp.bfloat16)

    def pack(g):
        layers = exchanged(field[g].astype(jnp.float32), field[4 + g].astype(jnp.float32))
        for half in range(2):
            planes[0, g, half, rows(c), :] = layers[half].astype(jnp.bfloat16)

    loads[0].wait()
    pack(0)
    pl.semaphore_wait(barrier, nc - 1 + has_prev.astype(jnp.int32) + has_next.astype(jnp.int32))
    send_own(0, 0)
    for g in range(1, GROUPS):
        pack(g)
        send_own(0, g)

    @pl.when(jnp.logical_not(has_prev))
    def _():
        for conv in range(2):
            for g in range(GROUPS):
                border_in[conv, g, 0] = jnp.zeros((local, LANES), jnp.bfloat16)

    @pl.when(jnp.logical_not(has_next))
    def _():
        for conv in range(2):
            for g in range(GROUPS):
                border_in[conv, g, 1] = jnp.zeros((local, LANES), jnp.bfloat16)

    loads[1].wait()
    loads[2].wait()
    bias1 = jnp.transpose(jnp.broadcast_to(b1[...], (LANES, local)))
    bias2 = jnp.transpose(jnp.broadcast_to(b2[...], (LANES, local)))
    loads[3].wait()
    for g in range(GROUPS):
        multiply_own(0, g, w1)
    for g in range(GROUPS):
        wait_chan(0, g)
        multiply_rest(0, g, w1)
        if g == 0:
            loads[4].wait()
        else:
            conclude(0, g - 1, bias1, keep)
            send_own(1, g - 1)
        if g > 1:
            multiply_own(1, g - 2, w2)
    multiply_own(1, GROUPS - 2, w2)
    conclude(0, GROUPS - 1, bias1, keep)
    send_own(1, GROUPS - 1)
    multiply_own(1, GROUPS - 1, w2)
    for g in range(GROUPS):
        wait_chan(1, g)
        multiply_rest(1, g, w2)
        if g > 0:
            conclude(1, g - 1, bias2, finish)
    conclude(1, GROUPS - 1, bias2, finish)
    for conv in range(2):
        for g in range(GROUPS):
            wait_sends(conv, g)


def per_device(ns, nc, field_in, kernel_first, bias_first, kernel_second, bias_second):
    layers, local, voxels = field_in.shape
    full = local * nc
    hbm = pl.BlockSpec(memory_space=pltpu.HBM)
    dma = pltpu.SemaphoreType.DMA
    border = pltpu.VMEM((2, GROUPS, 2, local, LANES), jnp.bfloat16)
    return pl.pallas_call(
        functools.partial(kernel, ns, nc),
        out_shape=jax.ShapeDtypeStruct(field_in.shape, jnp.bfloat16),
        in_specs=[hbm] * 5,
        out_specs=pl.BlockSpec(memory_space=pltpu.VMEM),
        scratch_shapes=[
            pltpu.VMEM((2, GROUPS, 2, full, LANES), jnp.bfloat16),
            pltpu.VMEM(kernel_first.shape, jnp.bfloat16),
            pltpu.VMEM(kernel_second.shape, jnp.bfloat16),
            pltpu.VMEM((GROUPS, 3, 2, 3, local, LANES), jnp.float32),
            pltpu.VMEM(field_in.shape, jnp.bfloat16),
            pltpu.VMEM((1, local), jnp.float32),
            pltpu.VMEM((1, local), jnp.float32),
            border,
            border,
            dma((5,)),
            dma((2, GROUPS, nc)),
            dma((2, GROUPS, nc)),
            dma((2, GROUPS, 2)),
            dma((2, GROUPS, 2)),
        ],
        cost_estimate=pl.CostEstimate(
            flops=2 * 2 * 27 * local * full * layers * voxels,
            bytes_accessed=2 * 27 * local * full * 2,
            transcendentals=2 * layers * local * voxels,
        ),
        compiler_params=pltpu.CompilerParams(
            collective_id=0, has_side_effects=True, vmem_limit_bytes=60 * 1024 * 1024
        ),
    )(field_in, kernel_first, bias_first.reshape(1, local), kernel_second, bias_second.reshape(1, local))


def solution(mesh):
    placed = (
        P("space", "chan", None),
        P(None, None, None, "chan", None),
        P("chan"),
        P(None, None, None, "chan", None),
        P("chan"),
    )
    body = functools.partial(per_device, mesh.shape["space"], mesh.shape["chan"])
    return jax.shard_map(
        body, mesh=mesh, in_specs=placed, out_specs=P("space", "chan", None), check_vma=False
    )
```
